256 devices in a mesh: dp: 32 (over x, z), code: 8 (over y, core).
Axes of the slice: x: 4, y: 4, z: 8, core: 2. Of those that a mesh axis runs over, the one named last changes fastest.
Arguments:
- frames: bfloat16 [24576, 1024], P('dp')
- prototypes: bfloat16 [32768, 1024], P(('dp', 'code'))
Outputs:
- updated: bfloat16 [32768, 1024], P(('dp', 'code'))
- log_scale: float32 [24576], P('dp')
All inputs are finite; a program needn't handle non-finite values.
Results may differ from the reference program's by a relative error of at most 0.0095.
Values may be sent and summed in bfloat16 or wider, within the bound.
A program may use at most 192 MiB of HBM per device.

```python
import math
import jax
import jax.numpy as jnp
from jax import lax

D = 1024
K = 32768
ITERS = 3
FRAMES = 24576
N_DP = 32


cluster_total = 256


def shared_protos(key):
    key_centers = jax.random.fold_in(key, 11)
    key_member = jax.random.fold_in(key, 12)
    key_cohesion = jax.random.fold_in(key, 13)
    key_own = jax.random.fold_in(key, 14)
    centers = jax.random.normal(key_centers, (cluster_total, D), jnp.float32)
    member_of = jax.random.randint(key_member, (K,), 0, cluster_total)
    cohesion = jax.random.uniform(key_cohesion, (cluster_total,), jnp.float32, 0.15, 0.6)
    picked = cohesion[member_of][:, None]
    own_noise = jax.random.normal(key_own, (K, D), jnp.float32)
    return jnp.sqrt(picked) * centers[member_of] + jnp.sqrt(1.0 - picked) * own_noise


def draw_prototypes(key, part):
    base = shared_protos(key)
    return base.astype(jnp.bfloat16)


def draw_frames(key, part):
    base = shared_protos(key)
    key = jax.random.fold_in(key, 2)
    key_selection, key_noise = jax.random.split(key, 2)
    chosen = jax.random.randint(key_selection, (FRAMES,), 0, K)
    strength = 0.7
    noise = jax.random.normal(key_noise, (FRAMES, D), jnp.float32)
    mixed = strength * base[chosen] + math.sqrt(1.0 - strength * strength) * noise
    return mixed.astype(jnp.bfloat16)


def setup_inputs(seed: int = 0) -> dict:
    seeds = jax.random.split(jax.random.key(seed), 3)
    return {
        "frames": draw_frames(jax.random.fold_in(seeds[2], 71), 0),
        "prototypes": draw_prototypes(jax.random.fold_in(seeds[2], 71), 0),
    }


sharpness_divisor = 0.05

def unit_rows(values):
    values_wide = values.astype(jnp.float32)
    return values_wide * lax.rsqrt(lax.optimization_barrier(jnp.mean(values_wide * values_wide, axis=1, keepdims=True)) + 1e-06) / math.sqrt(values.shape[1])

def reference(frames, prototypes):
    frame_count = frames.shape[0]
    proto_count = prototypes.shape[0]
    utterance_vector_length = unit_rows(frames).astype(jnp.bfloat16)
    proto_wide = unit_rows(prototypes)
    center_vector_length = proto_wide.astype(jnp.bfloat16)
    affinity_matrix = jnp.exp(lax.dot_general(utterance_vector_length, center_vector_length, (((1,), (1,)), ((), ())), preferred_element_type=jnp.float32) / sharpness_divisor)
    weight = jnp.full((frame_count,), 1.0 / frame_count, jnp.float32)
    balance = jnp.ones((proto_count,), jnp.float32)
    for iteration in range(ITERS):
        column = jnp.dot(weight, affinity_matrix, precision=lax.Precision.HIGHEST)
        balance = 1.0 / (proto_count * column)
        row_total = jnp.dot(affinity_matrix, balance, precision=lax.Precision.HIGHEST)
        weight = 1.0 / (frame_count * row_total)
    col_mass = frame_count * balance * jnp.dot(weight, affinity_matrix, precision=lax.Precision.HIGHEST)
    assign = (frame_count * weight[:, None] * affinity_matrix * balance[None, :]).astype(jnp.bfloat16)
    block_rows = frame_count // N_DP
    allocation_pieces = assign.reshape(N_DP, block_rows, proto_count)
    frame_blocks = utterance_vector_length.reshape(N_DP, block_rows, frames.shape[1])

    def add_block(total, pair):
        part_assign, part_frames = pair
        partial_sum = lax.dot_general(part_assign, part_frames, (((0,), (0,)), ((), ())), preferred_element_type=jnp.float32)
        rounded_values = lax.optimization_barrier(partial_sum.astype(jnp.bfloat16))
        return (total + rounded_values.astype(jnp.float32), None)
    pooled, unused = lax.scan(add_block, jnp.zeros((proto_count, frames.shape[1]), jnp.float32), (allocation_pieces, frame_blocks))
    updated = (math.sqrt(frames.shape[1]) * (0.5 * proto_wide + 0.5 * pooled / col_mass[:, None])).astype(jnp.bfloat16)
    return (updated, jnp.log(frame_count * weight))
```

```python
import functools

import jax
import jax.numpy as jnp
from jax import lax
from jax.experimental import pallas as pl
from jax.experimental.pallas import tpu as pltpu
from jax.sharding import PartitionSpec as P

MESH = pl.DeviceIdType.MESH
F32 = jnp.float32
BF16 = jnp.bfloat16

X, Y, Z = 4, 4, 8
D = 1024
K = 32768
F = 24576
ITERS = 3
FR = F // (X * Z)
PR = K // (X * Y * Z * 2)
NF = FR * X
NP = PR * Z
LT = NF // 128
QR = FR // 4
SR = QR // 2
HP = PR // 2

ORDER = (0, 1, 7, 2, 6, 3, 5, 4)
POS = {slot: position for position, slot in enumerate(ORDER)}


def place():
    dp = lax.axis_index("dp")
    code = lax.axis_index("code")
    return dp // Z, code // 2, lax.rem(dp, Z), lax.rem(code, 2)


def device(dx=0, dy=0, dz=0, dc=0):
    x, y, z, c = place()
    return {
        "dp": lax.rem(x + dx, X) * Z + lax.rem(z + dz, Z),
        "code": lax.rem(y + dy, Y) * 2 + lax.rem(c + dc, 2),
    }


PLANE = [(dx, dy) for dx in range(X) for dy in range(Y) if (dx, dy) != (0, 0)]


def unit_rows(values):
    wide = values.astype(F32)
    return wide * lax.rsqrt(jnp.sum(wide * wide, axis=1, keepdims=True) * (1.0 / D) + 1e-6) * (1.0 / 32.0)


def kernel(
    frames, protos, updated, log_scale,
    xn, pn, et, qb, pooled, cacc, bcol,
    csend, cslots, rpart, rsib, rslots, rwide, arow, brow,
    sbuf, rbuf,
    fx_recv, fy_recv, fs_recv, f_send, p_recv, p_send,
    c_recv, c_send, rs_recv, rs_send, r_recv, r_send, m_recv, m_send,
):
    x, y, z, c = place()
    barrier = pltpu.get_barrier_semaphore()
    partners = [dict(dz=e) for e in range(1, Z)] + [dict(dx=a, dy=b) for a, b in PLANE] + [dict(dc=1)]
    for where in partners:
        pl.semaphore_signal(barrier, inc=1, device_id=device(**where), device_id_type=MESH)

    pn[0:PR, :] = unit_rows(protos[...]).astype(BF16)

    def norm_body(i, _):
        rows = pl.ds(pl.multiple_of(i * 64, 64), 64)
        xn[rows, :] = unit_rows(frames[rows, :]).astype(BF16)
        return 0

    lax.fori_loop(0, FR // 64, norm_body, 0)
    pl.semaphore_wait(barrier, len(partners))

    def send(src, dst, send_sem, recv_sem, **where):
        pltpu.make_async_remote_copy(
            src_ref=src, dst_ref=dst, send_sem=send_sem, recv_sem=recv_sem,
            device_id=device(**where), device_id_type=MESH,
        ).start()

    def wait(ref, sem):
        pltpu.make_async_copy(ref, ref, sem).wait()

    parity = lax.rem(y, 2)
    mine = parity * 2 + c
    other = (1 - parity) * 2 + c

    def frame_rows(slot, quarter, sub):
        start = slot * FR + quarter * QR + sub * SR
        return xn.at[pl.ds(pl.multiple_of(start, 32), SR), :]

    def x_send(slot_from, slot_to, sub, dx):
        send(frame_rows(slot_from, mine, sub), frame_rows(slot_to, mine, sub), f_send, fx_recv.at[slot_to, sub], dx=dx)

    def y_send(slot, sub):
        up = (slot == 3) == (sub == 1)
        send(frame_rows(slot, mine, sub), frame_rows(slot, mine, sub), f_send, fy_recv.at[slot, sub], dy=1 if up else 3)

    def sib_send(slot, quarter, sub):
        send(frame_rows(slot, quarter, sub), frame_rows(slot, quarter, sub), f_send, fs_recv.at[slot], dc=1)

    def x_arrival(slot, sub):
        ref = frame_rows(slot, mine, sub)
        wait(ref, fx_recv.at[slot, sub])
        if slot == 1 and sub == 0:
            x_send(1, 2, 0, 3)
        if slot == 3 and sub == 1:
            x_send(3, 2, 1, 1)
        y_send(slot, sub)
        sib_send(slot, mine, sub)

    def y_arrival(slot, sub):
        wait(frame_rows(slot, other, sub), fy_recv.at[slot, sub])
        sib_send(slot, other, sub)

    def frames_done(slot):
        wait(xn.at[0 : 4 * SR, :], fs_recv.at[slot])

    def proto_rows(slot, sub):
        start = POS[slot] * PR + sub * HP
        return pn.at[start : start + HP, :]

    def p_hop(slot_from, slot_to, sub, dz):
        send(proto_rows(slot_from, sub), proto_rows(slot_to, sub), p_send, p_recv.at[slot_to, sub], dz=dz)

    def p_arrival(slot, sub):
        wait(proto_rows(slot, sub), p_recv.at[slot, sub])
        if slot in (1, 2) or (slot == 3 and sub == 0):
            p_hop(slot, slot + 1, sub, Z - 1)
        if slot in (7, 6) or (slot == 5 and sub == 1):
            p_hop(slot, slot - 1, sub, 1)

    for sub in range(2):
        x_send(0, 1, sub, 3)
        x_send(0, 3, sub, 1)
        p_hop(0, 1, sub, Z - 1)
        p_hop(0, 7, 1 - sub, 1)

    def score(row0, count, slot, first):
        rows = pl.ds(row0, count)
        columns = slice(slot * FR, (slot + 1) * FR)
        product = lax.dot_general(
            pn[rows, :], xn[columns, :], (((1,), (1,)), ((), ())), preferred_element_type=F32
        )
        value = jnp.exp(product * 20.0)
        et[rows, columns] = value
        part = value[:, 0:128]
        for j in range(1, FR // 128):
            part = part + value[:, j * 128 : (j + 1) * 128]
        if first:
            cacc[rows, :] = part
        else:
            cacc[rows, :] = cacc[rows, :] + part

    score(0, PR, 0, True)
    p_arrival(1, 0)
    p_arrival(7, 1)
    x_arrival(1, 0)
    x_arrival(3, 0)
    p_arrival(1, 1)
    p_arrival(7, 0)
    score(PR, 2 * PR, 0, True)
    x_arrival(1, 1)
    x_arrival(3, 1)
    p_arrival(2, 0)
    p_arrival(6, 1)
    y_arrival(1, 0)
    y_arrival(3, 0)
    p_arrival(2, 1)
    p_arrival(6, 0)
    score(3 * PR, 2 * PR, 0, True)
    x_arrival(2, 0)
    x_arrival(2, 1)
    p_arrival(3, 0)
    p_arrival(5, 1)
    y_arrival(1, 1)
    y_arrival(3, 1)
    frames_done(1)
    frames_done(3)
    for slot in (1, 3):
        score(0, PR, slot, False)
        score(PR, 2 * PR, slot, False)
    p_arrival(3, 1)
    p_arrival(5, 0)
    for slot in (1, 3):
        score(3 * PR, 2 * PR, slot, False)
    y_arrival(2, 0)
    y_arrival(2, 1)
    for slot in (0, 1, 3):
        score(5 * PR, 2 * PR, slot, slot == 0)
    p_arrival(4, 0)
    p_arrival(4, 1)
    for slot in (0, 1, 3):
        score(7 * PR, PR, slot, slot == 0)
    frames_done(2)

    def score_body(i, _):
        score(pl.multiple_of(i * 256, 256), 256, 2, False)
        return 0

    lax.fori_loop(0, NP // 256, score_body, 0)

    eye = lax.broadcasted_iota(jnp.int32, (128, 128), 0) == lax.broadcasted_iota(jnp.int32, (128, 128), 1)

    def column_start(k):
        for p in range(Z):
            column = jnp.sum(cacc[p * PR : (p + 1) * PR, :], axis=1, keepdims=True)
            csend[k, ORDER[p] : ORDER[p] + 1, :] = jnp.sum(jnp.where(eye, column, 0.0), axis=0, keepdims=True)
        for e in range(1, Z):
            send(csend.at[k], cslots.at[k, e - 1], c_send.at[k], c_recv.at[k], dz=e)

    def column_total(k):
        wait(cslots.at[k], c_recv.at[k])
        total = csend[k]
        for e in range(1, Z):
            total = total + pltpu.roll(cslots[k, e - 1], Z - e, 0)
        return total

    def to_column(row):
        return jnp.sum(jnp.where(eye, row, 0.0), axis=1, keepdims=True)

    def row_pass(k):
        def body(i, acc):
            acc = list(acc)
            for g in range(8):
                rows = pl.ds(pl.multiple_of(i * 64 + g * 8, 8), 8)
                weight = bcol[rows, :]
                for j in range(LT):
                    acc[j] = acc[j] + et[rows, j * 128 : (j + 1) * 128] * weight
            return tuple(acc)

        acc = lax.fori_loop(0, NP // 64, body, tuple(jnp.zeros((8, 128), F32) for _ in range(LT)))
        for j in range(LT):
            rpart[k, j : j + 1, :] = jnp.sum(acc[j], axis=0, keepdims=True)

    def row_total(k):
        send(rpart.at[k], rsib.at[k], rs_send.at[k], rs_recv.at[k], dc=1)
        wait(rsib.at[k], rs_recv.at[k])
        rslots[k, y] = rpart[k] + rsib[k]
        for dx, dy in PLANE:
            send(rslots.at[k, y], rslots.at[k, dx * Y + y], r_send.at[k], r_recv.at[k], dx=dx, dy=dy)
        wait(rslots.at[k, 0 : X * Y - 1], r_recv.at[k])
        total = None
        for dx in range(X):
            slots = [rslots[k, dx * Y + dy] for dy in range(Y)]
            part = (slots[0] + slots[1]) + (slots[2] + slots[3])
            if dx == 0:
                total = part
            else:
                rwide[0:LT, :] = part
                rwide[LT : 2 * LT, :] = part
                shift = dx * (FR // 128)
                total = total + rwide[shift : shift + LT, :]
        return total

    def column_pass():
        weights = [jnp.broadcast_to(arow[j : j + 1, :], (8, 128)) for j in range(LT)]

        def body(i, _):
            for g in range(8):
                rows = pl.ds(pl.multiple_of(i * 64 + g * 8, 8), 8)
                acc = [None] * 4
                for j in range(LT):
                    term = et[rows, j * 128 : (j + 1) * 128] * weights[j]
                    acc[j % 4] = term if acc[j % 4] is None else acc[j % 4] + term
                cacc[rows, :] = (acc[0] + acc[1]) + (acc[2] + acc[3])
            return 0

        lax.fori_loop(0, NP // 64, body, 0)

    def last_pass():
        weights = [jnp.broadcast_to(arow[j : j + 1, :] * float(F), (16, 128)) for j in range(LT)]

        def body(i, _):
            for g in range(4):
                rows = pl.ds(pl.multiple_of(i * 64 + g * 16, 16), 16)
                acc = [None] * 2
                for j in range(LT):
                    columns = slice(j * 128, (j + 1) * 128)
                    term = et[rows, columns] * weights[j]
                    qb[rows, columns] = term.astype(BF16)
                    acc[j % 2] = term if acc[j % 2] is None else acc[j % 2] + term
                cacc[rows, :] = acc[0] + acc[1]
            return 0

        lax.fori_loop(0, NP // 64, body, 0)

    for k in range(ITERS):
        column_start(k)
        total = column_total(k)
        if k == 0:
            total = total * (1.0 / F)
        brow[...] = 1.0 / (float(K) * total)
        for p in range(Z):
            bcol[p * PR : (p + 1) * PR, :] = jnp.broadcast_to(
                to_column(brow[ORDER[p] : ORDER[p] + 1, :]), (PR, 128)
            )
        row_pass(k)
        arow[...] = 1.0 / (float(F) * row_total(k))
        if k < ITERS - 1:
            column_pass()
    last_pass()
    column_start(ITERS)
    log_scale[...] = jnp.log(float(F) * arow[0:8, :])

    def pool(position, count):
        rows = slice(position * PR, (position + count) * PR)

        def body(n, _):
            columns = pl.ds(pl.multiple_of(n * 256, 256), 256)
            pooled[rows, columns] = jnp.dot(qb[rows, :], xn[:, columns], preferred_element_type=F32)
            return 0

        lax.fori_loop(0, D // 256, body, 0)

    def hop(way, step, sub):
        slot = 4 - step if way == 0 else 4 + step
        start = POS[slot] * PR + sub * HP
        value = pooled[start : start + HP, :]
        if step > 1 or (step == 1 and sub == way):
            before = slice((step - 1) * PR + sub * HP, (step - 1) * PR + (sub + 1) * HP)
            wait(rbuf.at[way, before, :], m_recv.at[way, step - 1, sub])
            value = value + rbuf[way, before, :].astype(F32)
        half = slice(step * PR + sub * HP, step * PR + (sub + 1) * HP)
        sbuf[way, half, :] = value.astype(BF16)
        send(
            sbuf.at[way, half, :], rbuf.at[way, half, :],
            m_send.at[way], m_recv.at[way, step, sub], dz=1 if way == 0 else Z - 1,
        )

    pool(POS[4], 1)
    hop(0, 0, 0)
    hop(1, 0, 1)
    pool(POS[3], 2)
    hop(0, 1, 1)
    hop(1, 1, 0)
    pool(POS[2], 2)
    hop(0, 1, 0)
    hop(1, 1, 1)
    pool(POS[1], 2)
    for step in (2, 3):
        if step == 3:
            pool(0, 1)
        for turn in range(2):
            hop(0, step, 1 - turn)
            hop(1, step, turn)

    mass = brow[0:1, :] * column_total(ITERS)[0:1, :]
    scale_column = to_column(brow[0:1, :] / mass)
    wide = unit_rows(protos[...])
    for turn in range(2):
        for way in range(2):
            sub = 1 - turn if way == 0 else turn
            half = slice(3 * PR + sub * HP, 3 * PR + (sub + 1) * HP)
            wait(rbuf.at[way, half, :], m_recv.at[way, 3, sub])
    last = slice(3 * PR, 4 * PR)
    own = pooled[0:PR, :] + rbuf[0, last, :].astype(F32) + rbuf[1, last, :].astype(F32)
    updated[...] = (32.0 * (0.5 * wide + 0.5 * (own * scale_column))).astype(BF16)

    wait(xn.at[0 : 24 * SR, :], f_send)
    wait(pn.at[0 : 14 * HP, :], p_send)
    for k in range(ITERS + 1):
        wait(cslots.at[k], c_send.at[k])
    for k in range(ITERS):
        wait(rsib.at[k], rs_send.at[k])
        wait(rslots.at[k, 0 : X * Y - 1], r_send.at[k])
    for way in range(2):
        wait(sbuf.at[way, 0 : 7 * HP, :], m_send.at[way])


def per_device(frames, prototypes):
    vmem = pl.BlockSpec(memory_space=pltpu.VMEM)
    dma = pltpu.SemaphoreType.DMA
    updated, log_scale = pl.pallas_call(
        kernel,
        out_shape=(jax.ShapeDtypeStruct((PR, D), BF16), jax.ShapeDtypeStruct((8, 128), F32)),
        in_specs=[vmem, vmem],
        out_specs=(vmem, vmem),
        scratch_shapes=[
            pltpu.VMEM((NF, D), BF16),
            pltpu.VMEM((NP, D), BF16),
            pltpu.VMEM((NP, NF), F32),
            pltpu.VMEM((NP, NF), BF16),
            pltpu.VMEM((NP, D), F32),
            pltpu.VMEM((NP, 128), F32),
            pltpu.VMEM((NP, 128), F32),
            pltpu.VMEM((ITERS + 1, Z, 128), F32),
            pltpu.VMEM((ITERS + 1, Z - 1, Z, 128), F32),
            pltpu.VMEM((ITERS, LT, 128), F32),
            pltpu.VMEM((ITERS, LT, 128), F32),
            pltpu.VMEM((ITERS, X * Y, LT, 128), F32),
            pltpu.VMEM((2 * LT, 128), F32),
            pltpu.VMEM((LT, 128), F32),
            pltpu.VMEM((Z, 128), F32),
            pltpu.VMEM((2, 4 * PR, D), BF16),
            pltpu.VMEM((2, 4 * PR, D), BF16),
            dma((4, 2)), dma((4, 2)), dma((4,)), dma,
            dma((Z, 2)), dma,
            dma((ITERS + 1,)), dma((ITERS + 1,)),
            dma((ITERS,)), dma((ITERS,)), dma((ITERS,)), dma((ITERS,)),
            dma((2, 4, 2)), dma((2,)),
        ],
        compiler_params=pltpu.CompilerParams(
            collective_id=0, has_side_effects=True, vmem_limit_bytes=56 * 2**20
        ),
    )(frames, prototypes)
    return updated, log_scale[0 : FR // 128].reshape(FR)


def solution(mesh):
    return jax.shard_map(
        per_device,
        mesh=mesh,
        in_specs=(P("dp", None), P(("dp", "code"), None)),
        out_specs=(P(("dp", "code"), None), P("dp")),
        check_vma=False,
    )
```

```python
import functools

import jax
import jax.numpy as jnp
from jax import lax
from jax.experimental import pallas as pl
from jax.experimental.pallas import tpu as pltpu
from jax.sharding import PartitionSpec as P

MESH = pl.DeviceIdType.MESH
F32 = jnp.float32
BF16 = jnp.bfloat16

X, Y, Z = 4, 4, 8
D = 1024
K = 32768
F = 24576
ITERS = 3
FR = F // (X * Z)
PR = K // (X * Y * Z * 2)
NF = FR * X
NP = PR * Z
LT = NF // 128
QR = FR // 4
SUBS = 4
SR = QR // SUBS
HP = PR // SUBS
CW = D // SUBS
RC = LT // 8

ORDER = (0, 1, 7, 2, 6, 3, 5, 4)
POS = {slot: position for position, slot in enumerate(ORDER)}
TURNS = {0: (2, 3, 0, 1), 1: (0, 1, 2, 3)}
NEAR = [dict(dx=1), dict(dx=X - 1), dict(dy=1), dict(dy=Y - 1), dict(dz=1), dict(dz=Z - 1), dict(dc=1)]
ROUNDS = 3


def place():
    dp = lax.axis_index("dp")
    code = lax.axis_index("code")
    return dp // Z, code // 2, lax.rem(dp, Z), lax.rem(code, 2)


def device(dx=0, dy=0, dz=0, dc=0):
    x, y, z, c = place()
    return {
        "dp": lax.rem(x + dx, X) * Z + lax.rem(z + dz, Z),
        "code": lax.rem(y + dy, Y) * 2 + lax.rem(c + dc, 2),
    }


def ring(step, size):
    return min(step, size - step)


PLANE = sorted(
    [(dx, dy) for dx in range(X) for dy in range(Y) if (dx, dy) != (0, 0)],
    key=lambda d: -ring(d[0], X) - ring(d[1], Y),
)
LINE = sorted(range(1, Z), key=lambda e: -ring(e, Z))


def unit_rows(values):
    wide = values.astype(F32)
    return wide * lax.rsqrt(jnp.sum(wide * wide, axis=1, keepdims=True) * (1.0 / D) + 1e-6) * (1.0 / 32.0)


def kernel(
    frames_hbm, protos_hbm, updated, log_scale,
    frames, protos, xn, pn, et, qb, pooled, cacc, bcol,
    csend, cslots, rpart, rsib, rslots, rwide, arow, brow, base,
    sbuf, rbuf,
    in_sem, hop_sem,
    fx_recv, fy_recv, fs_recv, f_send, p_recv, p_send,
    c_recv, c_send, rs_recv, rs_send, r_recv, r_send, m_recv, m_send,
):
    x, y, z, c = place()
    protos_in = pltpu.make_async_copy(protos_hbm, protos, in_sem.at[0])
    frames_in = pltpu.make_async_copy(frames_hbm, frames, in_sem.at[1])
    protos_in.start()
    frames_in.start()
    barrier = pltpu.get_barrier_semaphore()
    for where in NEAR:
        pl.semaphore_signal(barrier, inc=1, device_id=device(**where), device_id_type=MESH)

    protos_in.wait()
    base[...] = unit_rows(protos[...])
    pn[0:PR, :] = base[...].astype(BF16)
    frames_in.wait()

    def norm_body(i, _):
        rows = pl.ds(pl.multiple_of(i * 64, 64), 64)
        xn[rows, :] = unit_rows(frames[rows, :]).astype(BF16)
        return 0

    lax.fori_loop(0, FR // 64, norm_body, 0)
    pl.semaphore_wait(barrier, len(NEAR))

    def tell(r):
        for where in NEAR:
            pl.semaphore_signal(hop_sem.at[r], inc=1, device_id=device(**where), device_id_type=MESH)

    def hear(r):
        pl.semaphore_wait(hop_sem.at[r], len(NEAR))

    def send(src, dst, send_sem, recv_sem, **where):
        pltpu.make_async_remote_copy(
            src_ref=src, dst_ref=dst, send_sem=send_sem, recv_sem=recv_sem,
            device_id=device(**where), device_id_type=MESH,
        ).start()

    def wait(ref, sem):
        pltpu.make_async_copy(ref, ref, sem).wait()

    parity = lax.rem(y, 2)
    mine = parity * 2 + c
    other = (1 - parity) * 2 + c

    def frame_rows(slot, quarter, sub):
        start = slot * FR + quarter * QR + sub * SR
        return xn.at[pl.ds(pl.multiple_of(start, 16), SR), :]

    def x_send(slot_from, slot_to, sub, dx):
        send(frame_rows(slot_from, mine, sub), frame_rows(slot_to, mine, sub), f_send, fx_recv.at[slot_to, sub], dx=dx)

    def y_send(slot, sub, up):
        send(frame_rows(slot, mine, sub), frame_rows(slot, mine, sub), f_send, fy_recv.at[slot, sub], dy=1 if up else Y - 1)

    def sib_send(slot, quarter, sub):
        send(frame_rows(slot, quarter, sub), frame_rows(slot, quarter, sub), f_send, fs_recv.at[slot], dc=1)

    def x_arrival(turn):
        if turn < SUBS:
            pieces = [(1, TURNS[1][turn], turn % 2 == 0), (3, TURNS[0][turn], turn % 2 == 1)]
        else:
            pieces = [(2, TURNS[1][turn - SUBS], True), (2, TURNS[0][turn - SUBS], False)]
        for slot, sub, up in pieces:
            wait(frame_rows(slot, mine, sub), fx_recv.at[slot, sub])
            if turn < 2:
                if slot == 1:
                    x_send(1, 2, sub, X - 1)
                else:
                    x_send(3, 2, sub, 1)
            y_send(slot, sub, up)
            sib_send(slot, mine, sub)

    def y_arrival(turn):
        if turn < SUBS:
            pieces = [(1, TURNS[1][turn]), (3, TURNS[0][turn])]
        else:
            pieces = [(2, TURNS[1][turn - SUBS]), (2, TURNS[0][turn - SUBS])]
        for slot, sub in pieces:
            wait(frame_rows(slot, other, sub), fy_recv.at[slot, sub])
            sib_send(slot, other, sub)

    def frames_done(slot):
        wait(xn.at[0 : 2 * SUBS * SR, :], fs_recv.at[slot])

    def proto_rows(slot, sub):
        start = POS[slot] * PR + sub * HP
        return pn.at[start : start + HP, :]

    def p_hop(slot_from, slot_to, sub, dz):
        send(proto_rows(slot_from, sub), proto_rows(slot_to, sub), p_send, p_recv.at[slot_to, sub], dz=dz)

    def p_arrival(hop, turn):
        if hop == 4:
            for way in range(2):
                sub = TURNS[way][turn]
                wait(proto_rows(4, sub), p_recv.at[4, sub])
            return
        for way, slot in ((1, hop), (0, Z - hop)):
            sub = TURNS[way][turn]
            wait(proto_rows(slot, sub), p_recv.at[slot, sub])
            if hop < 3 or turn < 2:
                p_hop(slot, slot + 1 if way == 1 else slot - 1, sub, Z - 1 if way == 1 else 1)

    for turn in range(SUBS):
        x_send(0, 1, TURNS[1][turn], X - 1)
        x_send(0, 3, TURNS[0][turn], 1)
        p_hop(0, 1, TURNS[1][turn], Z - 1)
        p_hop(0, 7, TURNS[0][turn], 1)
    tell(0)

    def score(position, count, column, width):
        rows = slice(position * PR, (position + count) * PR)
        columns = slice(column, column + width)
        product = lax.dot_general(
            pn[rows, :], xn[columns, :], (((1,), (1,)), ((), ())), preferred_element_type=F32
        )
        value = jnp.exp(product * 20.0)
        et[rows, columns] = value
        part = value[:, 0:128]
        for j in range(1, width // 128):
            part = part + value[:, j * 128 : (j + 1) * 128]
        if column == 0:
            cacc[rows, :] = part
        else:
            cacc[rows, :] = cacc[rows, :] + part

    score(0, 1, 0, FR)
    p_arrival(1, 0)
    x_arrival(0)
    p_arrival(1, 1)
    hear(0)
    tell(1)
    p_arrival(1, 2)
    x_arrival(1)
    p_arrival(1, 3)
    score(1, 2, 0, FR)
    x_arrival(2)
    p_arrival(2, 0)
    y_arrival(0)
    hear(1)
    tell(2)
    p_arrival(2, 1)
    x_arrival(3)
    y_arrival(1)
    p_arrival(2, 2)
    x_arrival(4)
    p_arrival(2, 3)
    y_arrival(2)
    score(3, 2, 0, FR)
    p_arrival(3, 0)
    x_arrival(5)
    y_arrival(3)
    hear(2)
    p_arrival(3, 1)
    frames_done(1)
    frames_done(3)
    score(0, 5, FR, 256)
    score(0, 5, FR + 256, 256)
    p_arrival(3, 2)
    y_arrival(4)
    score(0, 5, FR + 512, 256)
    score(0, 5, 3 * FR, 256)
    p_arrival(3, 3)
    y_arrival(5)
    score(0, 5, 3 * FR + 256, 256)
    score(0, 5, 3 * FR + 512, 256)
    for slot in (0, 1, 3):
        score(5, 2, slot * FR, FR)
    frames_done(2)
    for n in range(3):
        score(0, 7, 2 * FR + n * 256, 256)
    p_arrival(4, 0)
    p_arrival(4, 1)
    for slot in range(X):
        score(7, 1, slot * FR, FR)

    eye = lax.broadcasted_iota(jnp.int32, (128, 128), 0) == lax.broadcasted_iota(jnp.int32, (128, 128), 1)

    def column_start(k):
        for p in range(Z):
            column = jnp.sum(cacc[p * PR : (p + 1) * PR, :], axis=1, keepdims=True)
            csend[k, ORDER[p] : ORDER[p] + 1, :] = jnp.sum(jnp.where(eye, column, 0.0), axis=0, keepdims=True)
        for e in LINE:
            send(csend.at[k], cslots.at[k, e - 1], c_send.at[k], c_recv.at[k], dz=e)

    def column_total(k):
        wait(cslots.at[k], c_recv.at[k])
        total = csend[k]
        for e in range(1, Z):
            total = total + pltpu.roll(cslots[k, e - 1], Z - e, 0)
        return total

    def to_column(row):
        return jnp.sum(jnp.where(eye, row, 0.0), axis=1, keepdims=True)

    def row_pass(k):
        for j in range(RC):
            def body(i, acc):
                acc = list(acc)
                for g in range(8):
                    rows = pl.ds(pl.multiple_of(i * 64 + g * 8, 8), 8)
                    weight = bcol[rows, :]
                    for t in range(8):
                        at = (g % 2) * 8 + t
                        acc[at] = acc[at] + et[rows, (j * 8 + t) * 128 : (j * 8 + t + 1) * 128] * weight
                return tuple(acc)

            acc = lax.fori_loop(0, NP // 64, body, tuple(jnp.zeros((8, 128), F32) for _ in range(16)))
            for t in range(8):
                rpart[k, j, t : t + 1, :] = jnp.sum(acc[t] + acc[8 + t], axis=0, keepdims=True)
            send(rpart.at[k, j], rsib.at[k, j], rs_send.at[k, j], rs_recv.at[k, j], dc=1)

    def row_total(k):
        for j in range(RC):
            wait(rsib.at[k, j], rs_recv.at[k, j])
            rslots[k, j, y] = rpart[k, j] + rsib[k, j]
            for dx, dy in PLANE:
                send(
                    rslots.at[k, j, y], rslots.at[k, j, dx * Y + y], r_send.at[k, j], r_recv.at[k, j], dx=dx, dy=dy
                )
        for j in range(RC):
            wait(rslots.at[k, j, 0 : X * Y - 1], r_recv.at[k, j])
            for dx in range(X):
                slots = [rslots[k, j, dx * Y + dy] for dy in range(Y)]
                part = (slots[0] + slots[1]) + (slots[2] + slots[3])
                rwide[dx, j * 8 : (j + 1) * 8, :] = part
                if dx > 0:
                    rwide[dx, LT + j * 8 : LT + (j + 1) * 8, :] = part
        total = rwide[0, 0:LT, :]
        for dx in range(1, X):
            shift = dx * (FR // 128)
            total = total + rwide[dx, shift : shift + LT, :]
        return total

    def column_pass():
        weights = [jnp.broadcast_to(arow[j : j + 1, :], (8, 128)) for j in range(LT)]

        def body(i, _):
            for g in range(8):
                rows = pl.ds(pl.multiple_of(i * 64 + g * 8, 8), 8)
                acc = [None] * 4
                for j in range(LT):
                    term = et[rows, j * 128 : (j + 1) * 128] * weights[j]
                    acc[j % 4] = term if acc[j % 4] is None else acc[j % 4] + term
                cacc[rows, :] = (acc[0] + acc[1]) + (acc[2] + acc[3])
            return 0

        lax.fori_loop(0, NP // 64, body, 0)

    def last_pass(position, count):
        weights = [jnp.broadcast_to(arow[j : j + 1, :] * float(F), (16, 128)) for j in range(LT)]

        def body(i, _):
            for g in range(4):
                rows = pl.ds(pl.multiple_of(position * PR + i * 64 + g * 16, 16), 16)
                acc = [None] * 2
                for j in range(LT):
                    columns = slice(j * 128, (j + 1) * 128)
                    term = et[rows, columns] * weights[j]
                    qb[rows, columns] = term.astype(BF16)
                    acc[j % 2] = term if acc[j % 2] is None else acc[j % 2] + term
                cacc[rows, :] = acc[0] + acc[1]
            return 0

        lax.fori_loop(0, count * PR // 64, body, 0)

    for k in range(ITERS):
        column_start(k)
        total = column_total(k)
        if k == 0:
            total = total * (1.0 / F)
        brow[...] = 1.0 / (float(K) * total)
        for p in range(Z):
            bcol[p * PR : (p + 1) * PR, :] = jnp.broadcast_to(
                to_column(brow[ORDER[p] : ORDER[p] + 1, :]), (PR, 128)
            )
        row_pass(k)
        arow[...] = 1.0 / (float(F) * row_total(k))
        if k < ITERS - 1:
            column_pass()

    def pool(position, count, sub):
        rows = slice(position * PR, (position + count) * PR)
        columns = slice(sub * CW, (sub + 1) * CW)
        pooled[rows, columns] = jnp.dot(qb[rows, :], xn[:, columns], preferred_element_type=F32)

    def hop(way, step, sub):
        slot = 4 - step if way == 0 else 4 + step
        start = POS[slot] * PR
        value = pooled[start : start + PR, sub * CW : (sub + 1) * CW]
        if step > 1 or (step == 1 and sub in TURNS[1 - way][0:2]):
            wait(rbuf.at[way, (step - 1) * SUBS + sub], m_recv.at[way, step - 1, sub])
            value = value + rbuf[way, (step - 1) * SUBS + sub].astype(F32)
        sbuf[way, step * SUBS + sub] = value.astype(BF16)
        send(
            sbuf.at[way, step * SUBS + sub], rbuf.at[way, step * SUBS + sub],
            m_send.at[way], m_recv.at[way, step, sub], dz=1 if way == 0 else Z - 1,
        )

    last_pass(POS[4], 1)
    for turn in (2, 3):
        for way in range(2):
            sub = TURNS[way][turn]
            pool(POS[4], 1, sub)
            hop(way, 0, sub)
    last_pass(POS[3], 2)
    for turn in range(2):
        for way in range(2):
            sub = TURNS[way][turn]
            pool(POS[3], 2, sub)
            hop(way, 1, sub)
    last_pass(0, 5)
    hop(0, 1, TURNS[0][2])
    hop(1, 1, TURNS[1][2])
    column_start(ITERS)
    log_scale[...] = jnp.log(float(F) * arow[0:8, :])
    hop(0, 1, TURNS[0][3])
    hop(1, 1, TURNS[1][3])
    for step in (2, 3):
        for turn in range(2):
            for way in range(2):
                sub = TURNS[way][turn]
                pool(POS[4 - step], 2, sub)
                hop(way, step, sub)
        for turn in range(2, 4):
            hop(0, step, TURNS[0][turn])
            hop(1, step, TURNS[1][turn])
    for sub in range(SUBS):
        pool(0, 1, sub)

    mass = brow[0:1, :] * column_total(ITERS)[0:1, :]
    scale_column = to_column(brow[0:1, :] / mass)
    for sub in (2, 0, 3, 1):
        columns = slice(sub * CW, (sub + 1) * CW)
        own = pooled[0:PR, columns]
        for way in range(2):
            wait(rbuf.at[way, 3 * SUBS + sub], m_recv.at[way, 3, sub])
            own = own + rbuf[way, 3 * SUBS + sub].astype(F32)
        updated[:, columns] = (32.0 * (0.5 * base[:, columns] + 0.5 * (own * scale_column))).astype(BF16)

    wait(xn.at[0 : 12 * SUBS * SR, :], f_send)
    wait(pn.at[0 : 7 * SUBS * HP, :], p_send)
    for k in range(ITERS + 1):
        wait(cslots.at[k], c_send.at[k])
    for k in range(ITERS):
        for j in range(RC):
            wait(rsib.at[k, j], rs_send.at[k, j])
            wait(rslots.at[k, j, 0 : X * Y - 1], r_send.at[k, j])
    for way in range(2):
        wait(sbuf.at[way, 0 : 14], m_send.at[way])


def per_device(frames, prototypes):
    hbm = pl.BlockSpec(memory_space=pl.ANY)
    vmem = pl.BlockSpec(memory_space=pltpu.VMEM)
    dma = pltpu.SemaphoreType.DMA
    updated, log_scale = pl.pallas_call(
        kernel,
        out_shape=(jax.ShapeDtypeStruct((PR, D), BF16), jax.ShapeDtypeStruct((8, 128), F32)),
        in_specs=[hbm, hbm],
        out_specs=(vmem, vmem),
        scratch_shapes=[
            pltpu.VMEM((FR, D), BF16),
            pltpu.VMEM((PR, D), BF16),
            pltpu.VMEM((NF, D), BF16),
            pltpu.VMEM((NP, D), BF16),
            pltpu.VMEM((NP, NF), F32),
            pltpu.VMEM((NP, NF), BF16),
            pltpu.VMEM((NP, D), F32),
            pltpu.VMEM((NP, 128), F32),
            pltpu.VMEM((NP, 128), F32),
            pltpu.VMEM((ITERS + 1, Z, 128), F32),
            pltpu.VMEM((ITERS + 1, Z - 1, Z, 128), F32),
            pltpu.VMEM((ITERS, RC, 8, 128), F32),
            pltpu.VMEM((ITERS, RC, 8, 128), F32),
            pltpu.VMEM((ITERS, RC, X * Y, 8, 128), F32),
            pltpu.VMEM((X, 2 * LT, 128), F32),
            pltpu.VMEM((LT, 128), F32),
            pltpu.VMEM((Z, 128), F32),
            pltpu.VMEM((PR, D), F32),
            pltpu.VMEM((2, 4 * SUBS, PR, CW), BF16),
            pltpu.VMEM((2, 4 * SUBS, PR, CW), BF16),
            dma((2,)), pltpu.SemaphoreType.REGULAR((ROUNDS,)),
            dma((X, SUBS)), dma((X, SUBS)), dma((X,)), dma,
            dma((Z, SUBS)), dma,
            dma((ITERS + 1,)), dma((ITERS + 1,)),
            dma((ITERS, RC)), dma((ITERS, RC)), dma((ITERS, RC)), dma((ITERS, RC)),
            dma((2, 4, SUBS)), dma((2,)),
        ],
        compiler_params=pltpu.CompilerParams(
            collective_id=0, has_side_effects=True, vmem_limit_bytes=56 * 2**20
        ),
    )(frames, prototypes)
    return updated, log_scale[0 : FR // 128].reshape(FR)


def solution(mesh):
    return jax.shard_map(
        per_device,
        mesh=mesh,
        in_specs=(P("dp", None), P(("dp", "code"), None)),
        out_specs=(P(("dp", "code"), None), P("dp")),
        check_vma=False,
    )
```

```python
import functools

import jax
import jax.numpy as jnp
from jax import lax
from jax.experimental import pallas as pl
from jax.experimental.pallas import tpu as pltpu
from jax.sharding import PartitionSpec as P

MESH = pl.DeviceIdType.MESH
F32 = jnp.float32
BF16 = jnp.bfloat16

X, Y, Z = 4, 4, 8
D = 1024
K = 32768
F = 24576
ITERS = 3
FR = F // (X * Z)
PR = K // (X * Y * Z * 2)
NF = FR * X
NP = PR * Z
LT = NF // 128
QR = FR // 4
SUBS = 4
SR = QR // SUBS
HP = PR // SUBS
CW = D // SUBS
RC = LT // 8

ORDER = (0, 1, 7, 2, 6, 3, 5, 4)
POS = {slot: position for position, slot in enumerate(ORDER)}
SUBPOS = (0, 2, 1, 3)
TURNS = {0: (2, 3, 0, 1), 1: (0, 1, 2, 3)}
NEAR = [dict(dx=1), dict(dx=X - 1), dict(dy=1), dict(dy=Y - 1), dict(dz=1), dict(dz=Z - 1), dict(dc=1)]
ROUNDS = 4


def place():
    dp = lax.axis_index("dp")
    code = lax.axis_index("code")
    return dp // Z, code // 2, lax.rem(dp, Z), lax.rem(code, 2)


def neighbours():
    x, y, z, c = place()
    xs = [lax.rem(x + d, X) * Z for d in range(X)]
    ys = [lax.rem(y + d, Y) * 2 for d in range(Y)]
    zs = [lax.rem(z + d, Z) for d in range(Z)]
    cs = [c, 1 - c]

    def device(dx=0, dy=0, dz=0, dc=0):
        return {"dp": xs[dx] + zs[dz], "code": ys[dy] + cs[dc]}

    return device


def ring(step, size):
    return min(step, size - step)


PLANE = sorted(
    [(dx, dy, dc) for dx in range(X) for dy in range(Y) for dc in range(2) if (dx, dy, dc) != (0, 0, 0)],
    key=lambda d: -ring(d[0], X) - ring(d[1], Y),
)
LINE = sorted(range(1, Z), key=lambda e: -ring(e, Z))


def unit_rows(values):
    wide = values.astype(F32)
    return wide * lax.rsqrt(jnp.sum(wide * wide, axis=1, keepdims=True) * (1.0 / D) + 1e-6) * (1.0 / 32.0)


def kernel(
    frames_hbm, protos_hbm, updated, log_scale,
    frames, protos, xn, pn, et, qb, pooled, cacc, bcol,
    csend, cslots, rslots, rwide, arow, brow, base,
    sbuf, rbuf,
    in_sem, hop_sem,
    fx_recv, fy_recv, fs_recv, f_send, p_recv, p_send,
    c_recv, c_send, r_recv, r_send, m_recv, m_send,
):
    x, y, z, c = place()
    device = neighbours()
    protos_in = pltpu.make_async_copy(protos_hbm, protos, in_sem.at[0])
    frames_in = pltpu.make_async_copy(frames_hbm, frames, in_sem.at[1])
    protos_in.start()
    frames_in.start()
    barrier = pltpu.get_barrier_semaphore()
    for where in NEAR:
        pl.semaphore_signal(barrier, inc=1, device_id=device(**where), device_id_type=MESH)

    protos_in.wait()
    base[...] = unit_rows(protos[...])
    pn[0:PR, :] = base[...].astype(BF16)
    frames_in.wait()

    def norm_body(i, _):
        rows = pl.ds(pl.multiple_of(i * 64, 64), 64)
        xn[rows, :] = unit_rows(frames[rows, :]).astype(BF16)
        return 0

    lax.fori_loop(0, FR // 64, norm_body, 0)
    pl.semaphore_wait(barrier, len(NEAR))

    def tell(r):
        for where in NEAR:
            pl.semaphore_signal(hop_sem.at[r], inc=1, device_id=device(**where), device_id_type=MESH)

    def hear(r):
        pl.semaphore_wait(hop_sem.at[r], len(NEAR))

    def send(src, dst, send_sem, recv_sem, **where):
        pltpu.make_async_remote_copy(
            src_ref=src, dst_ref=dst, send_sem=send_sem, recv_sem=recv_sem,
            device_id=device(**where), device_id_type=MESH,
        ).start()

    def wait(ref, sem):
        pltpu.make_async_copy(ref, ref, sem).wait()

    parity = lax.rem(y, 2)
    mine = parity * 2 + c
    other = (1 - parity) * 2 + c

    def frame_rows(slot, quarter, sub):
        start = slot * FR + SUBPOS[sub] * QR + quarter * SR
        return xn.at[pl.ds(pl.multiple_of(start, 16), SR), :]

    def x_send(slot_from, slot_to, sub, dx):
        send(frame_rows(slot_from, mine, sub), frame_rows(slot_to, mine, sub), f_send, fx_recv.at[slot_to, sub], dx=dx)

    def y_send(slot, sub, up):
        send(frame_rows(slot, mine, sub), frame_rows(slot, mine, sub), f_send, fy_recv.at[slot, sub], dy=1 if up else Y - 1)

    def sib_send(slot, quarter, sub):
        send(frame_rows(slot, quarter, sub), frame_rows(slot, quarter, sub), f_send, fs_recv.at[slot, sub % 2 if slot == 2 else 0], dc=1)

    def x_arrival(turn):
        if turn < SUBS:
            pieces = [(1, TURNS[1][turn], turn % 2 == 0), (3, TURNS[0][turn], turn % 2 == 1)]
        else:
            pieces = [(2, TURNS[1][turn - SUBS], True), (2, TURNS[0][turn - SUBS], False)]
        for slot, sub, up in pieces:
            wait(frame_rows(slot, mine, sub), fx_recv.at[slot, sub])
            if turn < 2:
                if slot == 1:
                    x_send(1, 2, sub, X - 1)
                else:
                    x_send(3, 2, sub, 1)
            y_send(slot, sub, up)
            sib_send(slot, mine, sub)

    def y_arrival(turn):
        if turn < SUBS:
            pieces = [(1, TURNS[1][turn]), (3, TURNS[0][turn])]
        else:
            pieces = [(2, TURNS[1][turn - SUBS]), (2, TURNS[0][turn - SUBS])]
        for slot, sub in pieces:
            wait(frame_rows(slot, other, sub), fy_recv.at[slot, sub])
            sib_send(slot, other, sub)

    def frames_done(slot, half=0):
        count = SUBS if slot == 2 else 2 * SUBS
        wait(xn.at[0 : count * SR, :], fs_recv.at[slot, half])

    def proto_rows(slot, sub):
        start = POS[slot] * PR + sub * HP
        return pn.at[start : start + HP, :]

    def p_hop(slot_from, slot_to, sub, dz):
        send(proto_rows(slot_from, sub), proto_rows(slot_to, sub), p_send, p_recv.at[slot_to, sub], dz=dz)

    def p_arrival(hop, turn):
        if hop == 4:
            for way in range(2):
                sub = TURNS[way][turn]
                wait(proto_rows(4, sub), p_recv.at[4, sub])
            return
        for way, slot in ((1, hop), (0, Z - hop)):
            sub = TURNS[way][turn]
            wait(proto_rows(slot, sub), p_recv.at[slot, sub])
            if hop < 3 or turn < 2:
                p_hop(slot, slot + 1 if way == 1 else slot - 1, sub, Z - 1 if way == 1 else 1)

    for turn in range(SUBS):
        x_send(0, 1, TURNS[1][turn], X - 1)
        x_send(0, 3, TURNS[0][turn], 1)
        p_hop(0, 1, TURNS[1][turn], Z - 1)
        p_hop(0, 7, TURNS[0][turn], 1)
    tell(0)

    def score(position, count, column, width):
        rows = slice(position * PR, (position + count) * PR)
        columns = slice(column, column + width)
        product = lax.dot_general(
            pn[rows, :], xn[columns, :], (((1,), (1,)), ((), ())), preferred_element_type=F32
        )
        value = jnp.exp(product * 20.0)
        et[rows, columns] = value
        part = value[:, 0:128]
        for j in range(1, width // 128):
            part = part + value[:, j * 128 : (j + 1) * 128]
        if column == 0:
            cacc[rows, :] = part
        else:
            cacc[rows, :] = cacc[rows, :] + part

    score(0, 1, 0, FR)
    p_arrival(1, 0)
    x_arrival(0)
    p_arrival(1, 1)
    hear(0)
    tell(1)
    p_arrival(1, 2)
    x_arrival(1)
    p_arrival(1, 3)
    score(1, 2, 0, FR)
    x_arrival(2)
    p_arrival(2, 0)
    y_arrival(0)
    hear(1)
    tell(2)
    p_arrival(2, 1)
    x_arrival(3)
    y_arrival(1)
    p_arrival(2, 2)
    x_arrival(4)
    p_arrival(2, 3)
    y_arrival(2)
    score(3, 2, 0, FR)
    p_arrival(3, 0)
    x_arrival(5)
    y_arrival(3)
    hear(2)
    tell(3)
    p_arrival(3, 1)
    frames_done(1)
    frames_done(3)
    score(0, 5, FR, 256)
    score(0, 5, FR + 256, 256)
    p_arrival(3, 2)
    y_arrival(4)
    score(0, 5, FR + 512, 256)
    score(0, 5, 3 * FR, 256)
    p_arrival(3, 3)
    y_arrival(5)
    hear(3)
    score(0, 5, 3 * FR + 256, 256)
    score(0, 5, 3 * FR + 512, 256)
    for slot in (0, 1, 3):
        score(5, 2, slot * FR, FR)
    p_arrival(4, 0)
    p_arrival(4, 1)
    for slot in (0, 1, 3):
        score(7, 1, slot * FR, FR)
    frames_done(2, 0)
    score(0, 8, 2 * FR, 256)
    frames_done(2, 1)
    score(0, 8, 2 * FR + 256, 256)
    score(0, 8, 2 * FR + 512, 256)

    eye = lax.broadcasted_iota(jnp.int32, (128, 128), 0) == lax.broadcasted_iota(jnp.int32, (128, 128), 1)

    def column_start(k):
        for p in range(Z):
            column = jnp.sum(cacc[p * PR : (p + 1) * PR, :], axis=1, keepdims=True)
            csend[k, ORDER[p] : ORDER[p] + 1, :] = jnp.sum(jnp.where(eye, column, 0.0), axis=0, keepdims=True)
        for e in LINE:
            send(csend.at[k], cslots.at[k, e - 1], c_send.at[k], c_recv.at[k], dz=e)

    def column_total(k):
        wait(cslots.at[k], c_recv.at[k])
        total = csend[k]
        for e in range(1, Z):
            total = total + pltpu.roll(cslots[k, e - 1], Z - e, 0)
        return total

    def to_column(row):
        return jnp.sum(jnp.where(eye, row, 0.0), axis=1, keepdims=True)

    def row_pass(k):
        for j in range(RC):
            def body(i, acc):
                acc = list(acc)
                for g in range(8):
                    rows = pl.ds(pl.multiple_of(i * 64 + g * 8, 8), 8)
                    weight = bcol[rows, :]
                    for t in range(8):
                        at = (g % 2) * 8 + t
                        acc[at] = acc[at] + et[rows, (j * 8 + t) * 128 : (j * 8 + t + 1) * 128] * weight
                return tuple(acc)

            acc = lax.fori_loop(0, NP // 64, body, tuple(jnp.zeros((8, 128), F32) for _ in range(16)))
            for t in range(8):
                rslots[k, j, y * 2 + c, t : t + 1, :] = jnp.sum(acc[t] + acc[8 + t], axis=0, keepdims=True)
            for dx, dy, dc in PLANE:
                send(
                    rslots.at[k, j, y * 2 + c], rslots.at[k, j, dx * Y * 2 + y * 2 + c],
                    r_send.at[k, j], r_recv.at[k, j], dx=dx, dy=dy, dc=dc,
                )

    def row_total(k):
        for j in range(RC):
            wait(rslots.at[k, j, 0 : X * Y * 2 - 1], r_recv.at[k, j])
            for dx in range(X):
                slots = [rslots[k, j, dx * Y * 2 + i] for i in range(Y * 2)]
                while len(slots) > 1:
                    slots = [slots[i] + slots[i + 1] for i in range(0, len(slots), 2)]
                part = slots[0]
                rwide[dx, j * 8 : (j + 1) * 8, :] = part
                if dx > 0:
                    rwide[dx, LT + j * 8 : LT + (j + 1) * 8, :] = part
        total = rwide[0, 0:LT, :]
        for dx in range(1, X):
            shift = dx * (FR // 128)
            total = total + rwide[dx, shift : shift + LT, :]
        return total

    def column_pass():
        weights = [jnp.broadcast_to(arow[j : j + 1, :], (8, 128)) for j in range(LT)]

        def body(i, _):
            for g in range(8):
                rows = pl.ds(pl.multiple_of(i * 64 + g * 8, 8), 8)
                acc = [None] * 4
                for j in range(LT):
                    term = et[rows, j * 128 : (j + 1) * 128] * weights[j]
                    acc[j % 4] = term if acc[j % 4] is None else acc[j % 4] + term
                cacc[rows, :] = (acc[0] + acc[1]) + (acc[2] + acc[3])
            return 0

        lax.fori_loop(0, NP // 64, body, 0)

    def last_pass(position, count):
        weights = [jnp.broadcast_to(arow[j : j + 1, :] * float(F), (16, 128)) for j in range(LT)]

        def body(i, _):
            for g in range(4):
                rows = pl.ds(pl.multiple_of(position * PR + i * 64 + g * 16, 16), 16)
                acc = [None] * 2
                for j in range(LT):
                    columns = slice(j * 128, (j + 1) * 128)
                    term = et[rows, columns] * weights[j]
                    qb[rows, columns] = term.astype(BF16)
                    acc[j % 2] = term if acc[j % 2] is None else acc[j % 2] + term
                cacc[rows, :] = acc[0] + acc[1]
            return 0

        lax.fori_loop(0, count * PR // 64, body, 0)

    for k in range(ITERS):
        column_start(k)
        total = column_total(k)
        if k == 0:
            total = total * (1.0 / F)
        brow[...] = 1.0 / (float(K) * total)
        for p in range(Z):
            bcol[p * PR : (p + 1) * PR, :] = jnp.broadcast_to(
                to_column(brow[ORDER[p] : ORDER[p] + 1, :]), (PR, 128)
            )
        row_pass(k)
        arow[...] = 1.0 / (float(F) * row_total(k))
        if k < ITERS - 1:
            column_pass()

    def pool(position, count, sub):
        rows = slice(position * PR, (position + count) * PR)
        columns = slice(sub * CW, (sub + 1) * CW)
        pooled[rows, columns] = jnp.dot(qb[rows, :], xn[:, columns], preferred_element_type=F32)

    def hop(way, step, sub):
        slot = 4 - step if way == 0 else 4 + step
        start = POS[slot] * PR
        value = pooled[start : start + PR, sub * CW : (sub + 1) * CW]
        if step > 1 or (step == 1 and sub in TURNS[1 - way][0:2]):
            wait(rbuf.at[way, (step - 1) * SUBS + sub], m_recv.at[way, step - 1, sub])
            value = value + rbuf[way, (step - 1) * SUBS + sub].astype(F32)
        sbuf[way, step * SUBS + sub] = value.astype(BF16)
        send(
            sbuf.at[way, step * SUBS + sub], rbuf.at[way, step * SUBS + sub],
            m_send.at[way], m_recv.at[way, step, sub], dz=1 if way == 0 else Z - 1,
        )

    last_pass(POS[4], 1)
    for turn in (2, 3):
        for way in range(2):
            sub = TURNS[way][turn]
            pool(POS[4], 1, sub)
            hop(way, 0, sub)
    last_pass(POS[3], 2)
    for turn in range(2):
        for way in range(2):
            sub = TURNS[way][turn]
            pool(POS[3], 2, sub)
            hop(way, 1, sub)
    for step in (1, 2):
        last_pass(POS[3 - step], 2)
        for turn in range(2):
            for way in range(2):
                hop(way, step, TURNS[way][turn + 2])
            if turn == 0 and step == 2:
                last_pass(0, 1)
                column_start(ITERS)
                log_scale[...] = jnp.log(float(F) * arow[0:8, :])
        for turn in range(2):
            for way in range(2):
                sub = TURNS[way][turn]
                pool(POS[3 - step], 2, sub)
                hop(way, step + 1, sub)
    for turn in range(2):
        hop(0, 3, TURNS[0][turn + 2])
        hop(1, 3, TURNS[1][turn + 2])
    for sub in range(SUBS):
        pool(0, 1, sub)

    mass = brow[0:1, :] * column_total(ITERS)[0:1, :]
    scale_column = to_column(brow[0:1, :] / mass)
    for sub in (2, 0, 3, 1):
        columns = slice(sub * CW, (sub + 1) * CW)
        own = pooled[0:PR, columns]
        for way in range(2):
            wait(rbuf.at[way, 3 * SUBS + sub], m_recv.at[way, 3, sub])
            own = own + rbuf[way, 3 * SUBS + sub].astype(F32)
        updated[:, columns] = (32.0 * (0.5 * base[:, columns] + 0.5 * (own * scale_column))).astype(BF16)

    wait(xn.at[0 : 12 * SUBS * SR, :], f_send)
    wait(pn.at[0 : 7 * SUBS * HP, :], p_send)
    for k in range(ITERS + 1):
        wait(cslots.at[k], c_send.at[k])
    for k in range(ITERS):
        for j in range(RC):
            wait(rslots.at[k, j, 0 : X * Y * 2 - 1], r_send.at[k, j])
    for way in range(2):
        wait(sbuf.at[way, 0 : 14], m_send.at[way])


def finish(updated, log_scale, updated_out, log_scale_out):
    updated_out[...] = updated[...]
    for j in range(FR // 128):
        log_scale_out[j * 128 : (j + 1) * 128] = log_scale[j, :]


def per_device(frames, prototypes):
    hbm = pl.BlockSpec(memory_space=pl.ANY)
    vmem = pl.BlockSpec(memory_space=pltpu.VMEM)
    dma = pltpu.SemaphoreType.DMA
    updated, log_scale = pl.pallas_call(
        kernel,
        out_shape=(jax.ShapeDtypeStruct((PR, D), BF16), jax.ShapeDtypeStruct((8, 128), F32)),
        in_specs=[hbm, hbm],
        out_specs=(vmem, vmem),
        scratch_shapes=[
            pltpu.VMEM((FR, D), BF16),
            pltpu.VMEM((PR, D), BF16),
            pltpu.VMEM((NF, D), BF16),
            pltpu.VMEM((NP, D), BF16),
            pltpu.VMEM((NP, NF), F32),
            pltpu.VMEM((NP, NF), BF16),
            pltpu.VMEM((NP, D), F32),
            pltpu.VMEM((NP, 128), F32),
            pltpu.VMEM((NP, 128), F32),
            pltpu.VMEM((ITERS + 1, Z, 128), F32),
            pltpu.VMEM((ITERS + 1, Z - 1, Z, 128), F32),
            pltpu.VMEM((ITERS, RC, X * Y * 2, 8, 128), F32),
            pltpu.VMEM((X, 2 * LT, 128), F32),
            pltpu.VMEM((LT, 128), F32),
            pltpu.VMEM((Z, 128), F32),
            pltpu.VMEM((PR, D), F32),
            pltpu.VMEM((2, 4 * SUBS, PR, CW), BF16),
            pltpu.VMEM((2, 4 * SUBS, PR, CW), BF16),
            dma((2,)), pltpu.SemaphoreType.REGULAR((ROUNDS,)),
            dma((X, SUBS)), dma((X, SUBS)), dma((X, 2)), dma,
            dma((Z, SUBS)), dma,
            dma((ITERS + 1,)), dma((ITERS + 1,)),
            dma((ITERS, RC)), dma((ITERS, RC)),
            dma((2, 4, SUBS)), dma((2,)),
        ],
        compiler_params=pltpu.CompilerParams(
            collective_id=0, has_side_effects=True, vmem_limit_bytes=56 * 2**20
        ),
    )(frames, prototypes)
    return pl.pallas_call(
        finish,
        out_shape=(jax.ShapeDtypeStruct((PR, D), BF16), jax.ShapeDtypeStruct((FR,), F32)),
        in_specs=[vmem, vmem],
        out_specs=(vmem, vmem),
    )(updated, log_scale)


def solution(mesh):
    return jax.shard_map(
        per_device,
        mesh=mesh,
        in_specs=(P("dp", None), P(("dp", "code"), None)),
        out_specs=(P(("dp", "code"), None), P("dp")),
        check_vma=False,
    )
```

```python
import functools

import jax
import jax.numpy as jnp
from jax import lax
from jax.experimental import pallas as pl
from jax.experimental.pallas import tpu as pltpu
from jax.sharding import PartitionSpec as P

MESH = pl.DeviceIdType.MESH
F32 = jnp.float32
BF16 = jnp.bfloat16

X, Y, Z = 4, 4, 8
D = 1024
K = 32768
F = 24576
ITERS = 3
FR = F // (X * Z)
PR = K // (X * Y * Z * 2)
NF = FR * X
NP = PR * Z
LT = NF // 128
QR = FR // 4
SUBS = 4
SR = QR // SUBS
HP = PR // SUBS
CW = D // SUBS
RC = LT // 8

ORDER = (0, 1, 7, 2, 6, 3, 5, 4)
POS = {slot: position for position, slot in enumerate(ORDER)}
SUBPOS = (0, 2, 1, 3)
TURNS = {0: (2, 3, 0, 1), 1: (0, 1, 2, 3)}
NEAR = [dict(dx=1), dict(dx=X - 1), dict(dy=1), dict(dy=Y - 1), dict(dz=1), dict(dz=Z - 1), dict(dc=1)]
ROUNDS = 4


def place():
    dp = lax.axis_index("dp")
    code = lax.axis_index("code")
    return dp // Z, code // 2, lax.rem(dp, Z), lax.rem(code, 2)


def neighbours():
    x, y, z, c = place()
    xs = [lax.rem(x + d, X) * Z for d in range(X)]
    ys = [lax.rem(y + d, Y) * 2 for d in range(Y)]
    zs = [lax.rem(z + d, Z) for d in range(Z)]
    cs = [c, 1 - c]

    def device(dx=0, dy=0, dz=0, dc=0):
        return {"dp": xs[dx] + zs[dz], "code": ys[dy] + cs[dc]}

    return device


def ring(step, size):
    return min(step, size - step)


PLANE = sorted(
    [(dx, dy, dc) for dx in range(X) for dy in range(Y) for dc in range(2) if (dx, dy, dc) != (0, 0, 0)],
    key=lambda d: -ring(d[0], X) - ring(d[1], Y),
)
LINE = sorted(range(1, Z), key=lambda e: -ring(e, Z))


def unit_rows(values):
    wide = values.astype(F32)
    return wide * lax.rsqrt(jnp.sum(wide * wide, axis=1, keepdims=True) * (1.0 / D) + 1e-6) * (1.0 / 32.0)


def kernel(
    frames_hbm, protos_hbm, updated, log_scale,
    frames, protos, xn, pn, et, qb, pooled, cacc, bcol,
    csend, cslots, rslots, rwide, arow, brow, base,
    sbuf, rbuf,
    in_sem, hop_sem,
    fx_recv, fy_recv, fs_recv, f_send, p_recv, p_send,
    c_recv, c_send, r_recv, r_send, m_recv, m_send,
):
    x, y, z, c = place()
    device = neighbours()
    protos_in = pltpu.make_async_copy(protos_hbm, protos, in_sem.at[0])
    frames_in = pltpu.make_async_copy(frames_hbm, frames, in_sem.at[1])
    protos_in.start()
    frames_in.start()
    barrier = pltpu.get_barrier_semaphore()
    for where in NEAR:
        pl.semaphore_signal(barrier, inc=1, device_id=device(**where), device_id_type=MESH)

    protos_in.wait()
    base[...] = unit_rows(protos[...])
    pn[0:PR, :] = base[...].astype(BF16)
    frames_in.wait()

    def norm_body(i, _):
        rows = pl.ds(pl.multiple_of(i * 64, 64), 64)
        xn[rows, :] = unit_rows(frames[rows, :]).astype(BF16)
        return 0

    lax.fori_loop(0, FR // 64, norm_body, 0)
    pl.semaphore_wait(barrier, len(NEAR))

    def tell(r):
        for where in NEAR:
            pl.semaphore_signal(hop_sem.at[r], inc=1, device_id=device(**where), device_id_type=MESH)

    def hear(r):
        pl.semaphore_wait(hop_sem.at[r], len(NEAR))

    def send(src, dst, send_sem, recv_sem, **where):
        pltpu.make_async_remote_copy(
            src_ref=src, dst_ref=dst, send_sem=send_sem, recv_sem=recv_sem,
            device_id=device(**where), device_id_type=MESH,
        ).start()

    def wait(ref, sem):
        pltpu.make_async_copy(ref, ref, sem).wait()

    parity = lax.rem(y, 2)
    mine = parity * 2 + c
    other = (1 - parity) * 2 + c

    def frame_rows(slot, quarter, sub):
        start = slot * FR + SUBPOS[sub] * QR + quarter * SR
        return xn.at[pl.ds(pl.multiple_of(start, 16), SR), :]

    def x_send(slot_from, slot_to, sub, dx):
        send(frame_rows(slot_from, mine, sub), frame_rows(slot_to, mine, sub), f_send, fx_recv.at[slot_to, sub], dx=dx)

    def y_send(slot, sub, up):
        send(frame_rows(slot, mine, sub), frame_rows(slot, mine, sub), f_send, fy_recv.at[slot, sub], dy=1 if up else Y - 1)

    def sib_send(slot, quarter, sub):
        send(frame_rows(slot, quarter, sub), frame_rows(slot, quarter, sub), f_send, fs_recv.at[slot, sub % 2 if slot == 2 else 0], dc=1)

    def x_arrival(turn):
        if turn < SUBS:
            pieces = [(1, TURNS[1][turn], turn % 2 == 0), (3, TURNS[0][turn], turn % 2 == 1)]
        else:
            pieces = [(2, TURNS[1][turn - SUBS], True), (2, TURNS[0][turn - SUBS], False)]
        for slot, sub, up in pieces:
            wait(frame_rows(slot, mine, sub), fx_recv.at[slot, sub])
            if turn < 2:
                if slot == 1:
                    x_send(1, 2, sub, X - 1)
                else:
                    x_send(3, 2, sub, 1)
            y_send(slot, sub, up)
            sib_send(slot, mine, sub)

    def y_arrival(turn):
        if turn < SUBS:
            pieces = [(1, TURNS[1][turn]), (3, TURNS[0][turn])]
        else:
            pieces = [(2, TURNS[1][turn - SUBS]), (2, TURNS[0][turn - SUBS])]
        for slot, sub in pieces:
            wait(frame_rows(slot, other, sub), fy_recv.at[slot, sub])
            sib_send(slot, other, sub)

    def frames_done(slot, half=0):
        count = SUBS if slot == 2 else 2 * SUBS
        wait(xn.at[0 : count * SR, :], fs_recv.at[slot, half])

    def proto_rows(slot, sub):
        start = POS[slot] * PR + sub * HP
        return pn.at[start : start + HP, :]

    def p_hop(slot_from, slot_to, sub, dz):
        send(proto_rows(slot_from, sub), proto_rows(slot_to, sub), p_send, p_recv.at[slot_to, sub], dz=dz)

    def p_arrival(hop, turn):
        if hop == 4:
            for way in range(2):
                sub = TURNS[way][turn]
                wait(proto_rows(4, sub), p_recv.at[4, sub])
            return
        for way, slot in ((1, hop), (0, Z - hop)):
            sub = TURNS[way][turn]
            wait(proto_rows(slot, sub), p_recv.at[slot, sub])
            if hop < 3 or turn < 2:
                p_hop(slot, slot + 1 if way == 1 else slot - 1, sub, Z - 1 if way == 1 else 1)

    for turn in range(SUBS):
        x_send(0, 1, TURNS[1][turn], X - 1)
        x_send(0, 3, TURNS[0][turn], 1)
        p_hop(0, 1, TURNS[1][turn], Z - 1)
        p_hop(0, 7, TURNS[0][turn], 1)
    tell(0)

    def score(position, count, column, width):
        rows = slice(position * PR, (position + count) * PR)
        columns = slice(column, column + width)
        product = lax.dot_general(
            pn[rows, :], xn[columns, :], (((1,), (1,)), ((), ())), preferred_element_type=F32
        )
        value = jnp.exp(product * 20.0)
        et[rows, columns] = value
        part = value[:, 0:128]
        for j in range(1, width // 128):
            part = part + value[:, j * 128 : (j + 1) * 128]
        if column == 0:
            cacc[rows, :] = part
        else:
            cacc[rows, :] = cacc[rows, :] + part

    score(0, 1, 0, FR)
    p_arrival(1, 0)
    x_arrival(0)
    p_arrival(1, 1)
    hear(0)
    tell(1)
    p_arrival(1, 2)
    x_arrival(1)
    p_arrival(1, 3)
    score(1, 2, 0, FR)
    x_arrival(2)
    p_arrival(2, 0)
    y_arrival(0)
    hear(1)
    tell(2)
    p_arrival(2, 1)
    x_arrival(3)
    y_arrival(1)
    p_arrival(2, 2)
    x_arrival(4)
    p_arrival(2, 3)
    y_arrival(2)
    score(3, 2, 0, FR)
    p_arrival(3, 0)
    x_arrival(5)
    y_arrival(3)
    hear(2)
    tell(3)
    p_arrival(3, 1)
    frames_done(1)
    frames_done(3)
    score(0, 5, FR, 256)
    score(0, 5, FR + 256, 256)
    p_arrival(3, 2)
    y_arrival(4)
    score(0, 5, FR + 512, 256)
    score(0, 5, 3 * FR, 256)
    p_arrival(3, 3)
    y_arrival(5)
    hear(3)
    score(0, 5, 3 * FR + 256, 256)
    score(0, 5, 3 * FR + 512, 256)
    score(5, 2, 0, FR)
    frames_done(2, 0)
    score(0, 5, 2 * FR, 256)
    p_arrival(4, 0)
    p_arrival(4, 1)
    score(7, 1, 0, FR)
    for slot in (1, 3):
        score(5, 3, slot * FR, FR)
    score(5, 3, 2 * FR, 256)
    frames_done(2, 1)
    score(0, 8, 2 * FR + 256, 256)
    score(0, 8, 2 * FR + 512, 256)

    eye = lax.broadcasted_iota(jnp.int32, (128, 128), 0) == lax.broadcasted_iota(jnp.int32, (128, 128), 1)

    def column_start(k):
        for p in range(Z):
            column = jnp.sum(cacc[p * PR : (p + 1) * PR, :], axis=1, keepdims=True)
            csend[k, ORDER[p] : ORDER[p] + 1, :] = jnp.sum(jnp.where(eye, column, 0.0), axis=0, keepdims=True)
        for e in LINE:
            send(csend.at[k], cslots.at[k, e - 1], c_send.at[k], c_recv.at[k], dz=e)

    def column_total(k):
        wait(cslots.at[k], c_recv.at[k])
        total = csend[k]
        for e in range(1, Z):
            total = total + pltpu.roll(cslots[k, e - 1], Z - e, 0)
        return total

    def to_column(row):
        return jnp.sum(jnp.where(eye, row, 0.0), axis=1, keepdims=True)

    def row_pass(k):
        for j in range(RC):
            def body(i, acc):
                acc = list(acc)
                for g in range(8):
                    rows = pl.ds(pl.multiple_of(i * 64 + g * 8, 8), 8)
                    weight = bcol[rows, :]
                    for t in range(8):
                        at = (g % 2) * 8 + t
                        acc[at] = acc[at] + et[rows, (j * 8 + t) * 128 : (j * 8 + t + 1) * 128] * weight
                return tuple(acc)

            acc = lax.fori_loop(0, NP // 64, body, tuple(jnp.zeros((8, 128), F32) for _ in range(16)))
            for t in range(8):
                rslots[k, j, y * 2 + c, t : t + 1, :] = jnp.sum(acc[t] + acc[8 + t], axis=0, keepdims=True)
            for dx, dy, dc in PLANE:
                send(
                    rslots.at[k, j, y * 2 + c], rslots.at[k, j, dx * Y * 2 + y * 2 + c],
                    r_send.at[k, j], r_recv.at[k, j], dx=dx, dy=dy, dc=dc,
                )

    def row_total(k):
        for j in range(RC):
            wait(rslots.at[k, j, 0 : X * Y * 2 - 1], r_recv.at[k, j])
            for dx in range(X):
                slots = [rslots[k, j, dx * Y * 2 + i] for i in range(Y * 2)]
                while len(slots) > 1:
                    slots = [slots[i] + slots[i + 1] for i in range(0, len(slots), 2)]
                part = slots[0]
                rwide[dx, j * 8 : (j + 1) * 8, :] = part
                if dx > 0:
                    rwide[dx, LT + j * 8 : LT + (j + 1) * 8, :] = part
        total = rwide[0, 0:LT, :]
        for dx in range(1, X):
            shift = dx * (FR // 128)
            total = total + rwide[dx, shift : shift + LT, :]
        return total

    def column_pass():
        weights = [jnp.broadcast_to(arow[j : j + 1, :], (8, 128)) for j in range(LT)]

        def body(i, _):
            for g in range(8):
                rows = pl.ds(pl.multiple_of(i * 64 + g * 8, 8), 8)
                acc = [None] * 4
                for j in range(LT):
                    term = et[rows, j * 128 : (j + 1) * 128] * weights[j]
                    acc[j % 4] = term if acc[j % 4] is None else acc[j % 4] + term
                cacc[rows, :] = (acc[0] + acc[1]) + (acc[2] + acc[3])
            return 0

        lax.fori_loop(0, NP // 64, body, 0)

    def last_pass(position, count):
        weights = [jnp.broadcast_to(arow[j : j + 1, :] * float(F), (16, 128)) for j in range(LT)]

        def body(i, _):
            for g in range(4):
                rows = pl.ds(pl.multiple_of(position * PR + i * 64 + g * 16, 16), 16)
                acc = [None] * 2
                for j in range(LT):
                    columns = slice(j * 128, (j + 1) * 128)
                    term = et[rows, columns] * weights[j]
                    qb[rows, columns] = term.astype(BF16)
                    acc[j % 2] = term if acc[j % 2] is None else acc[j % 2] + term
                cacc[rows, :] = acc[0] + acc[1]
            return 0

        lax.fori_loop(0, count * PR // 64, body, 0)

    for k in range(ITERS):
        column_start(k)
        total = column_total(k)
        if k == 0:
            total = total * (1.0 / F)
        brow[...] = 1.0 / (float(K) * total)
        for p in range(Z):
            bcol[p * PR : (p + 1) * PR, :] = jnp.broadcast_to(
                to_column(brow[ORDER[p] : ORDER[p] + 1, :]), (PR, 128)
            )
        row_pass(k)
        arow[...] = 1.0 / (float(F) * row_total(k))
        if k < ITERS - 1:
            column_pass()

    def pool(position, count, sub):
        rows = slice(position * PR, (position + count) * PR)
        columns = slice(sub * CW, (sub + 1) * CW)
        pooled[rows, columns] = jnp.dot(qb[rows, :], xn[:, columns], preferred_element_type=F32)

    def hop(way, step, sub):
        slot = 4 - step if way == 0 else 4 + step
        start = POS[slot] * PR
        value = pooled[start : start + PR, sub * CW : (sub + 1) * CW]
        if step > 1 or (step == 1 and sub in TURNS[1 - way][0:2]):
            wait(rbuf.at[way, (step - 1) * SUBS + sub], m_recv.at[way, step - 1, sub])
            value = value + rbuf[way, (step - 1) * SUBS + sub].astype(F32)
        sbuf[way, step * SUBS + sub] = value.astype(BF16)
        send(
            sbuf.at[way, step * SUBS + sub], rbuf.at[way, step * SUBS + sub],
            m_send.at[way], m_recv.at[way, step, sub], dz=1 if way == 0 else Z - 1,
        )

    last_pass(POS[4], 1)
    for turn in (2, 3):
        for way in range(2):
            sub = TURNS[way][turn]
            pool(POS[4], 1, sub)
            hop(way, 0, sub)
    last_pass(POS[3], 2)
    for turn in range(2):
        for way in range(2):
            sub = TURNS[way][turn]
            pool(POS[3], 2, sub)
            hop(way, 1, sub)
    for step in (1, 2):
        last_pass(POS[3 - step], 2)
        for turn in range(2):
            for way in range(2):
                hop(way, step, TURNS[way][turn + 2])
            if turn == 0 and step == 2:
                last_pass(0, 1)
                column_start(ITERS)
                log_scale[...] = jnp.log(float(F) * arow[0:8, :])
        for turn in range(2):
            for way in range(2):
                sub = TURNS[way][turn]
                pool(POS[3 - step], 2, sub)
                hop(way, step + 1, sub)
    for turn in range(2):
        hop(0, 3, TURNS[0][turn + 2])
        hop(1, 3, TURNS[1][turn + 2])
    for sub in range(SUBS):
        pool(0, 1, sub)

    mass = brow[0:1, :] * column_total(ITERS)[0:1, :]
    scale_column = to_column(brow[0:1, :] / mass)
    for sub in (2, 0, 3, 1):
        columns = slice(sub * CW, (sub + 1) * CW)
        own = pooled[0:PR, columns]
        for way in range(2):
            wait(rbuf.at[way, 3 * SUBS + sub], m_recv.at[way, 3, sub])
            own = own + rbuf[way, 3 * SUBS + sub].astype(F32)
        updated[:, columns] = (32.0 * (0.5 * base[:, columns] + 0.5 * (own * scale_column))).astype(BF16)

    wait(xn.at[0 : 12 * SUBS * SR, :], f_send)
    wait(pn.at[0 : 7 * SUBS * HP, :], p_send)
    for k in range(ITERS + 1):
        wait(cslots.at[k], c_send.at[k])
    for k in range(ITERS):
        for j in range(RC):
            wait(rslots.at[k, j, 0 : X * Y * 2 - 1], r_send.at[k, j])
    for way in range(2):
        wait(sbuf.at[way, 0 : 14], m_send.at[way])


def finish(updated, log_scale, updated_out, log_scale_out):
    updated_out[...] = updated[...]
    for j in range(FR // 128):
        log_scale_out[j * 128 : (j + 1) * 128] = log_scale[j, :]


def per_device(frames, prototypes):
    hbm = pl.BlockSpec(memory_space=pl.ANY)
    vmem = pl.BlockSpec(memory_space=pltpu.VMEM)
    dma = pltpu.SemaphoreType.DMA
    updated, log_scale = pl.pallas_call(
        kernel,
        out_shape=(jax.ShapeDtypeStruct((PR, D), BF16), jax.ShapeDtypeStruct((8, 128), F32)),
        in_specs=[hbm, hbm],
        out_specs=(vmem, vmem),
        scratch_shapes=[
            pltpu.VMEM((FR, D), BF16),
            pltpu.VMEM((PR, D), BF16),
            pltpu.VMEM((NF, D), BF16),
            pltpu.VMEM((NP, D), BF16),
            pltpu.VMEM((NP, NF), F32),
            pltpu.VMEM((NP, NF), BF16),
            pltpu.VMEM((NP, D), F32),
            pltpu.VMEM((NP, 128), F32),
            pltpu.VMEM((NP, 128), F32),
            pltpu.VMEM((ITERS + 1, Z, 128), F32),
            pltpu.VMEM((ITERS + 1, Z - 1, Z, 128), F32),
            pltpu.VMEM((ITERS, RC, X * Y * 2, 8, 128), F32),
            pltpu.VMEM((X, 2 * LT, 128), F32),
            pltpu.VMEM((LT, 128), F32),
            pltpu.VMEM((Z, 128), F32),
            pltpu.VMEM((PR, D), F32),
            pltpu.VMEM((2, 4 * SUBS, PR, CW), BF16),
            pltpu.VMEM((2, 4 * SUBS, PR, CW), BF16),
            dma((2,)), pltpu.SemaphoreType.REGULAR((ROUNDS,)),
            dma((X, SUBS)), dma((X, SUBS)), dma((X, 2)), dma,
            dma((Z, SUBS)), dma,
            dma((ITERS + 1,)), dma((ITERS + 1,)),
            dma((ITERS, RC)), dma((ITERS, RC)),
            dma((2, 4, SUBS)), dma((2,)),
        ],
        compiler_params=pltpu.CompilerParams(
            collective_id=0, has_side_effects=True, vmem_limit_bytes=56 * 2**20
        ),
    )(frames, prototypes)
    return pl.pallas_call(
        finish,
        out_shape=(jax.ShapeDtypeStruct((PR, D), BF16), jax.ShapeDtypeStruct((FR,), F32)),
        in_specs=[vmem, vmem],
        out_specs=(vmem, vmem),
    )(updated, log_scale)


def solution(mesh):
    return jax.shard_map(
        per_device,
        mesh=mesh,
        in_specs=(P("dp", None), P(("dp", "code"), None)),
        out_specs=(P(("dp", "code"), None), P("dp")),
        check_vma=False,
    )
```
